32 devices in a mesh: energy: 16 (over z, y, x), mom: 2 (over core).
Axes of the slice: x: 2, y: 2, z: 4, core: 2. Of those that a mesh axis runs over, the one named last changes fastest.
Arguments:
- lesser: bfloat16 [2, 2, 512, 65536], P('mom', None, 'energy'), may hold values from -6 to 6
- greater: bfloat16 [2, 2, 512, 65536], P('mom', None, 'energy'), may hold values from -6 to 6
- coulomb: bfloat16 [2, 4, 128, 128], P('mom'), may hold values from -0.375 to 0.375
- tile_block: int32 [4], replicated, may hold values from 0 to 3, each once
- shift_table: int32 [2, 2], replicated, may hold values from 0 to 1, each once within a row
Outputs:
- polarization: bfloat16 [2, 2, 512, 65536], P('mom', None, 'energy')
- screened: float32 [2, 2, 128, 65536], P('mom', None, 'energy')
The draws below stay inside these ranges and needn't reach their ends.
Inputs may be any that keep to these rules, and one draw needn't show every extreme that they name: `tile_block`: each of the 4 tiles holds a different block of the pattern. `shift_table`: each row names every momentum once.
All inputs are finite; a program needn't handle non-finite values.
Results may differ from the reference program's by a relative error of at most 0.0013.
Values may be sent and summed in bfloat16 or wider, within the bound.
No kernel may reach another device: no remote copies, remote signals or barrier semaphores. Data moves between devices by JAX's collectives and lax.ppermute only.
A program may use at most 256 MiB of HBM per device.

```python
import math
import jax
import jax.numpy as jnp
from jax import lax

E = 512
NK = 2
BS = 128
NBW = 2
NT = 4
NNZ = 65536


def levels(key, shape, split, low, largest):
    loudness, own = 1.0, jax.random.fold_in(key, 6)
    for axis_at, shards_of in split:
        heights = jnp.exp(jax.random.uniform(jax.random.fold_in(own, axis_at), (shards_of,), jnp.float32, low / len(split), largest / len(split)))
        loudness = loudness * jnp.repeat(heights, shape[axis_at] // shards_of).reshape([-1 if axis == axis_at else 1 for axis in range(len(shape))])
    return loudness


def normal_values(own_key, shape, scale, bound, pieces=(), held_as=jnp.bfloat16):
    factor_of = levels(own_key, shape, pieces, -0.22, 0.18) if pieces else 1.0
    array = jax.random.normal(own_key, shape, jnp.float32) * scale * factor_of
    return jnp.minimum(jnp.maximum(array, -bound), bound).astype(held_as)


def setup_inputs(seed: int = 0) -> dict:
    arg_keys = jax.random.split(jax.random.key(seed), 6)
    return {
        "lesser": normal_values(arg_keys[0], (NK, 2, E, NNZ), 1.0, 6.0, ((0, 2), (2, 16))),
        "greater": normal_values(arg_keys[1], (NK, 2, E, NNZ), 1.0, 6.0, ((0, 2), (2, 16))),
        "coulomb": normal_values(arg_keys[2], (NK, NT, BS, BS), (2 * BS) ** -0.5, 0.375, ((0, 2),)),
        "tile_block": jax.random.permutation(arg_keys[3], NT).astype(jnp.int32),
        "shift_table": jax.vmap(lambda own: jax.random.permutation(own, NK))(jax.random.split(arg_keys[4], NK)).reshape((NK, NK)).astype(jnp.int32),
    }


def pattern_blocks(count):
    return [(r, c) for r in range(count) for c in range(max(0, r - 1), min(count, r + 2))]

def polar_columns(lesser, greater, shift_table, start, width):
    left = lax.dynamic_slice_in_dim(lesser, start, width, 3).astype(jnp.float32)
    right = lax.dynamic_slice_in_dim(greater, start, width, 3).astype(jnp.float32)
    left_spec = jnp.fft.fft(lax.complex(left[:, 0], left[:, 1]), n=2 * E, axis=1)
    right_spec = jnp.fft.fft(lax.complex(right[:, 0], right[:, 1]), n=2 * E, axis=1)
    paired = jnp.take(right_spec, shift_table, axis=0)
    total = lax.optimization_barrier(jnp.sum(left_spec[None] * jnp.conj(paired), axis=1))
    corr = jnp.fft.ifft(total, axis=1)[:, :E]
    factor = 1.0 / math.sqrt(NK * E)
    return (jnp.stack([-jnp.imag(corr), jnp.real(corr)], axis=1) * factor).astype(jnp.float32)

def reference(lesser, greater, coulomb, tile_block, shift_table):
    width = min(NNZ, 4096)
    count = NNZ // width

    def one(index):
        return polar_columns(lesser, greater, shift_table, index * width, width)
    parts = lax.map(one, jnp.arange(count, dtype=jnp.int32))
    polar_full = jnp.transpose(parts, (1, 2, 3, 0, 4)).reshape(NK, 2, E, NNZ)
    polarization = polar_full.astype(jnp.bfloat16)
    leading = polarization[:, :, :E // 4].reshape(NK, 2, E // 4, NT, BS, BS)
    inverse = jnp.argsort(tile_block).astype(jnp.int32)
    ordered = jnp.take(leading, inverse, axis=3).astype(jnp.float32)
    weights = coulomb.astype(jnp.float32)
    results = []
    for r, c in pattern_blocks(NBW):
        acc = jnp.zeros((NK, 2, E // 4, BS, BS), jnp.float32)
        for l in range(max(0, r - 1), min(NBW, r + 2)):
            if abs(l - c) <= 1:
                acc = acc + jnp.einsum('qij,qsejk->qseik', weights[:, 2 * r + l], ordered[:, :, :, 2 * l + c])
        results.append(acc)
    screened = jnp.stack(results, axis=3).reshape(NK, 2, E // 4, NNZ)
    return (polarization, screened)
```

```python
import functools
import math

import jax
import jax.numpy as jnp
import ml_dtypes
import numpy as np
from jax import lax
from jax.experimental import pallas as pl
from jax.experimental.pallas import tpu as pltpu
from jax.sharding import PartitionSpec as P

AXES = ("energy", "mom")
LANES = 128


def split_table(table):
    high = table.astype(np.float32).astype(ml_dtypes.bfloat16)
    low = (table - high.astype(np.float64)).astype(np.float32).astype(ml_dtypes.bfloat16)
    return high, low


@functools.lru_cache(maxsize=None)
def tables(energies, scale):
    period = 2 * energies
    turns = (2 * np.arange(energies)[:, None] + 1) * np.arange(energies)[None, :] % (2 * period)
    angle = np.pi / period * turns
    forward = np.concatenate((np.cos(angle), -np.sin(angle)), axis=0)
    backward = np.concatenate((np.cos(angle).T, -np.sin(angle).T), axis=1) * (scale / period)
    f_high, f_low = split_table(forward)
    b_high, b_low = split_table(backward)
    return np.concatenate((f_high, f_low), axis=1), np.concatenate((b_high, b_low, b_high), axis=1)


def correlate_kernel(shift, forward, backward, data, out, spectra, packed):
    blocks, count, _, _, rows, width = data.shape
    energies = blocks * rows

    def spectrum(index, carry):
        k, side, part = index // 4, index // 2 % 2, index % 2
        column = data[:, k, side, part].reshape(energies, width)
        both = jnp.concatenate((column, column), axis=0)
        spectra[index] = jnp.dot(forward[...], both, preferred_element_type=jnp.float32)
        return carry

    lax.fori_loop(0, 4 * count, spectrum, 0)
    step = 16

    def multiply(index, carry):
        row = pl.multiple_of(index * step, step)

        def load(k, side):
            base = (k * 2 + side) * 2
            a_re = spectra[base, pl.ds(row, step)]
            a_im = spectra[base, pl.ds(energies + row, step)]
            b_re = spectra[base + 1, pl.ds(row, step)]
            b_im = spectra[base + 1, pl.ds(energies + row, step)]
            return a_re - b_im, a_im + b_re, a_re + b_im, a_im - b_re

        left = [load(k, 0) for k in range(count)]
        for q in range(count):
            p_re = p_im = m_re = m_im = 0.0
            for k in range(count):
                lu_re, lu_im, lv_re, lv_im = left[k]
                ru_re, ru_im, rv_re, rv_im = load(shift[q, k], 1)
                p_re = p_re + lu_re * ru_re + lu_im * ru_im
                p_im = p_im + lu_im * ru_re - lu_re * ru_im
                m_re = m_re + lv_re * rv_re + lv_im * rv_im
                m_im = m_im + lv_im * rv_re - lv_re * rv_im
            parts = ((m_im - p_im, p_re - m_re), (p_re + m_re, p_im + m_im))
            for part in range(2):
                for half in range(2):
                    value = parts[part][half]
                    high = value.astype(jnp.bfloat16)
                    low = (value - high.astype(jnp.float32)).astype(jnp.bfloat16)
                    packed[2 * q + part, pl.ds(half * energies + row, step)] = high
                    packed[2 * q + part, pl.ds((2 + half) * energies + row, step)] = high
                    packed[2 * q + part, pl.ds((4 + half) * energies + row, step)] = low
        return carry

    lax.fori_loop(0, energies // step, multiply, 0)

    def invert(index, carry):
        result = jnp.dot(backward[...], packed[index], preferred_element_type=jnp.float32)
        out[:, index // 2, index % 2] = result.astype(jnp.bfloat16).reshape(blocks, rows, width)
        return carry

    lax.fori_loop(0, 2 * count, invert, 0)


def correlate(data, shift_table, forward, backward):
    blocks, count, _, _, rows, columns = data.shape
    energies = blocks * rows
    width = 256 if columns % 256 == 0 else columns
    work = 2 * columns * energies * energies * (16 * count + 12 * count)
    return pl.pallas_call(
        correlate_kernel,
        grid=(columns // width,),
        in_specs=[
            pl.BlockSpec(memory_space=pltpu.SMEM),
            pl.BlockSpec(forward.shape, lambda i: (0, 0)),
            pl.BlockSpec(backward.shape, lambda i: (0, 0)),
            pl.BlockSpec((blocks, count, 2, 2, rows, width), lambda i: (0, 0, 0, 0, 0, i)),
        ],
        out_specs=pl.BlockSpec((blocks, count, 2, rows, width), lambda i: (0, 0, 0, 0, i)),
        out_shape=jax.ShapeDtypeStruct((blocks, count, 2, rows, columns), jnp.bfloat16),
        scratch_shapes=[
            pltpu.VMEM((4 * count, 2 * energies, width), jnp.float32),
            pltpu.VMEM((2 * count, 6 * energies, width), jnp.bfloat16),
        ],
        compiler_params=pltpu.CompilerParams(vmem_limit_bytes=48 * 2**20),
        cost_estimate=pl.CostEstimate(
            flops=work, bytes_accessed=data.size * 3, transcendentals=0
        ),
        name="correlate",
    )(shift_table, forward, backward, data)


def pack_kernel(lesser, greater, out):
    out[0, 0] = lesser[0]
    out[0, 1] = greater[0]


def pack(lesser, greater, start, width, devices):
    _, _, rows, _ = lesser.shape
    if rows % 16 or width % LANES or start % width:
        both = jnp.concatenate((lesser, greater), axis=0)[..., start : start + devices * width]
        return jnp.transpose(both.reshape(2, 2, rows, devices, width), (3, 0, 1, 2, 4))
    base = start // width
    spec = pl.BlockSpec((1, 2, rows, width), lambda i: (0, 0, 0, base + i))
    return pl.pallas_call(
        pack_kernel,
        grid=(devices,),
        in_specs=[spec, spec],
        out_specs=pl.BlockSpec((1, 2, 2, rows, width), lambda i: (i, 0, 0, 0, 0)),
        out_shape=jax.ShapeDtypeStruct((devices, 2, 2, rows, width), jnp.bfloat16),
        name="pack",
    )(lesser, greater)


def unpack_kernel(*refs):
    refs[-1][0] = refs[0][0]


def unpack(received, start, total, result):
    devices, _, rows, width = received.shape
    base = start // width
    more = {} if result is None else {"input_output_aliases": {1: 0}}
    held = [] if result is None else [result]
    return pl.pallas_call(
        unpack_kernel,
        grid=(devices,),
        in_specs=[pl.BlockSpec((1, 2, rows, width), lambda i: (i, 0, 0, 0))]
        + [pl.BlockSpec(memory_space=pl.ANY)] * len(held),
        out_specs=pl.BlockSpec((1, 2, rows, width), lambda i: (0, 0, 0, base + i)),
        out_shape=jax.ShapeDtypeStruct((1, 2, rows, total), jnp.bfloat16),
        name="unpack",
        **more,
    )(received, *held)


def exchange(array):
    return lax.all_to_all(array, AXES, split_axis=0, concat_axis=0, tiled=True)


def after(value, *earlier):
    return lax.optimization_barrier((value, *earlier))[0]


def screen(near, coulomb, tile_block):
    tiles_n, block = coulomb.shape[1], coulomb.shape[2]
    levels = near.shape[2]
    band = (tiles_n + 2) // 3
    tiles = near.reshape(tiles_n, block, 2, levels, block)
    labels = jnp.arange(tiles_n, dtype=jnp.int32)
    onehot = tile_block[:, None] == labels[None, :]
    inverse = jnp.sum(jnp.where(onehot, labels[:, None], 0), axis=0)
    ordered = jnp.take(tiles, inverse, axis=0)
    results = []
    for r in range(band):
        for c in range(max(0, r - 1), min(band, r + 2)):
            inner = [l for l in range(max(0, r - 1), min(band, r + 2)) if abs(l - c) <= 1]
            acc = sum(
                jnp.einsum(
                    "ij,jsek->seik",
                    coulomb[0, 2 * r + l],
                    ordered[2 * l + c],
                    preferred_element_type=jnp.float32,
                )
                for l in inner
            )
            results.append(acc)
    return jnp.stack(results, axis=2).reshape(1, 2, levels, tiles_n * block * block)


def shards(lesser, greater, coulomb, tile_block, shift_table):
    count = lax.axis_size("mom")
    groups = lax.axis_size("energy")
    devices = count * groups
    rows, total = lesser.shape[2:]
    energies = rows * groups
    leading = energies // 4 // groups
    block = coulomb.shape[2]
    columns = total // devices
    chunks = 2 if columns % (2 * LANES) == 0 else 1
    width = columns // chunks
    direct = rows % 16 == 0
    forward, backward = (jnp.asarray(t) for t in tables(energies, 1.0 / math.sqrt(count * energies)))

    received, previous = [], None
    for chunk in range(chunks):
        sent = pack(lesser, greater, chunk * devices * width, width, devices)
        if previous is not None:
            sent = after(sent, previous)
        previous = exchange(sent)
        received.append(previous)

    outs, firsts, polar = [], [], None
    for chunk in range(chunks):
        data = received[chunk].reshape(groups, count, 2, 2, rows, width)
        if not direct:
            data = jnp.transpose(data, (1, 2, 3, 0, 4, 5)).reshape(1, count, 2, 2, energies, width)
        polar = correlate(data, shift_table, forward, backward)
        if not direct:
            polar = polar.reshape(count, 2, groups, rows, width)
            polar = jnp.transpose(polar, (2, 0, 1, 3, 4))
        outs.append(polar.reshape(devices, 2, rows, width))
        if leading:
            head = jnp.transpose(polar[: groups // 4], (1, 2, 0, 3, 4))
            head = head.reshape(count, 2, groups, leading, width)
            firsts.append(jnp.transpose(head, (2, 0, 1, 3, 4)).reshape(devices, 2, leading, width))

    results = []
    for chunk in range(chunks):
        if chunk == chunks - 1:
            first = jnp.concatenate(firsts, axis=3)
            first = after(first, previous)
            previous = near = exchange(first)
        previous = exchange(after(outs[chunk], previous))
        results.append(previous)

    polarization = None
    for chunk in range(chunks):
        if direct:
            polarization = unpack(results[chunk], chunk * devices * width, total, polarization)
    if not direct:
        pieces = jnp.stack(results)
        polarization = jnp.transpose(pieces, (2, 3, 0, 1, 4)).reshape(1, 2, rows, total)
    near = near.reshape(devices, 2, leading, chunks, width // block, block)
    near = jnp.transpose(near, (3, 0, 4, 1, 2, 5)).reshape(total // block, 2, leading, block)
    return (polarization, screen(near, coulomb, tile_block))


def solution(mesh):
    return jax.shard_map(
        shards,
        mesh=mesh,
        in_specs=(
            P("mom", None, "energy", None),
            P("mom", None, "energy", None),
            P("mom", None, None, None),
            P(),
            P(),
        ),
        out_specs=(P("mom", None, "energy", None), P("mom", None, "energy", None)),
        check_vma=False,
    )
```

```python
import functools
import math

import jax
import jax.numpy as jnp
import ml_dtypes
import numpy as np
from jax import lax
from jax.experimental import pallas as pl
from jax.experimental.pallas import tpu as pltpu
from jax.sharding import PartitionSpec as P

AXES = ("energy", "mom")
LANES = 128


def split_table(table):
    high = table.astype(np.float32).astype(ml_dtypes.bfloat16)
    low = (table - high.astype(np.float64)).astype(np.float32).astype(ml_dtypes.bfloat16)
    return high, low


@functools.lru_cache(maxsize=None)
def tables(energies, scale):
    period = 2 * energies
    turns = (2 * np.arange(energies)[:, None] + 1) * np.arange(energies)[None, :] % (2 * period)
    angle = np.pi / period * turns
    forward = np.concatenate((np.cos(angle), -np.sin(angle)), axis=0)
    backward = np.concatenate((np.cos(angle).T, -np.sin(angle).T), axis=1) * (scale / period)
    f_high, f_low = split_table(forward)
    b_high, b_low = split_table(backward)
    return np.concatenate((f_high, f_low), axis=1), np.concatenate((b_high, b_low, b_high), axis=1)


def correlate_kernel(shift, forward, backward, data, out, spectra, packed):
    blocks, count, _, _, rows, width = data.shape
    energies = blocks * rows

    def spectrum(index, carry):
        k, side, part = index // 4, index // 2 % 2, index % 2
        column = data[:, k, side, part].reshape(energies, width)
        both = jnp.concatenate((column, column), axis=0)
        spectra[index] = jnp.dot(forward[...], both, preferred_element_type=jnp.float32)
        return carry

    lax.fori_loop(0, 4 * count, spectrum, 0)
    step = 16

    def multiply(index, carry):
        row = pl.multiple_of(index * step, step)

        def load(k, side):
            base = (k * 2 + side) * 2
            a_re = spectra[base, pl.ds(row, step)]
            a_im = spectra[base, pl.ds(energies + row, step)]
            b_re = spectra[base + 1, pl.ds(row, step)]
            b_im = spectra[base + 1, pl.ds(energies + row, step)]
            return a_re - b_im, a_im + b_re, a_re + b_im, a_im - b_re

        left = [load(k, 0) for k in range(count)]
        for q in range(count):
            p_re = p_im = m_re = m_im = 0.0
            for k in range(count):
                lu_re, lu_im, lv_re, lv_im = left[k]
                ru_re, ru_im, rv_re, rv_im = load(shift[q, k], 1)
                p_re = p_re + lu_re * ru_re + lu_im * ru_im
                p_im = p_im + lu_im * ru_re - lu_re * ru_im
                m_re = m_re + lv_re * rv_re + lv_im * rv_im
                m_im = m_im + lv_im * rv_re - lv_re * rv_im
            parts = ((m_im - p_im, p_re - m_re), (p_re + m_re, p_im + m_im))
            for part in range(2):
                for half in range(2):
                    value = parts[part][half]
                    high = value.astype(jnp.bfloat16)
                    low = (value - high.astype(jnp.float32)).astype(jnp.bfloat16)
                    packed[2 * q + part, pl.ds(half * energies + row, step)] = high
                    packed[2 * q + part, pl.ds((2 + half) * energies + row, step)] = high
                    packed[2 * q + part, pl.ds((4 + half) * energies + row, step)] = low
        return carry

    lax.fori_loop(0, energies // step, multiply, 0)

    def invert(index, carry):
        result = jnp.dot(backward[...], packed[index], preferred_element_type=jnp.float32)
        out[:, index // 2, index % 2] = result.astype(jnp.bfloat16).reshape(blocks, rows, width)
        return carry

    lax.fori_loop(0, 2 * count, invert, 0)


def correlate(data, shift_table, forward, backward):
    blocks, count, _, _, rows, columns = data.shape
    energies = blocks * rows
    width = 256 if columns % 256 == 0 else columns
    work = 2 * columns * energies * energies * (16 * count + 12 * count)
    return pl.pallas_call(
        correlate_kernel,
        grid=(columns // width,),
        in_specs=[
            pl.BlockSpec(memory_space=pltpu.SMEM),
            pl.BlockSpec(forward.shape, lambda i: (0, 0)),
            pl.BlockSpec(backward.shape, lambda i: (0, 0)),
            pl.BlockSpec((blocks, count, 2, 2, rows, width), lambda i: (0, 0, 0, 0, 0, i)),
        ],
        out_specs=pl.BlockSpec((blocks, count, 2, rows, width), lambda i: (0, 0, 0, 0, i)),
        out_shape=jax.ShapeDtypeStruct((blocks, count, 2, rows, columns), jnp.bfloat16),
        scratch_shapes=[
            pltpu.VMEM((4 * count, 2 * energies, width), jnp.float32),
            pltpu.VMEM((2 * count, 6 * energies, width), jnp.bfloat16),
        ],
        compiler_params=pltpu.CompilerParams(vmem_limit_bytes=48 * 2**20),
        cost_estimate=pl.CostEstimate(
            flops=work, bytes_accessed=data.size * 3, transcendentals=0
        ),
        name="correlate",
    )(shift_table, forward, backward, data)


def stage(pairs, arrived, left):
    inward = [
        pltpu.make_async_copy(source, buffer, arrived.at[index])
        for index, (source, buffer, _) in enumerate(pairs)
    ]
    outward = [
        pltpu.make_async_copy(buffer, target, left.at[index])
        for index, (_, buffer, target) in enumerate(pairs)
    ]
    for copy in inward:
        copy.start()
    for first, second in zip(inward, outward):
        first.wait()
        second.start()
    for copy in outward:
        copy.wait()


def pack_kernel(start, lesser, greater, out, buffer, arrived, left):
    devices, _, _, _, width = out.shape
    pairs = []
    for index in range(devices):
        columns = pl.ds(start + index * width, width)
        for side, array in enumerate((lesser, greater)):
            pairs.append((array.at[0, :, :, columns], buffer.at[index, side], out.at[index, side]))
    stage(pairs, arrived, left)


def pack(lesser, greater, start, width, devices):
    _, _, rows, _ = lesser.shape
    if rows % 16 or width % LANES or devices > 64:
        both = jnp.concatenate((lesser, greater), axis=0)[..., start : start + devices * width]
        return jnp.transpose(both.reshape(2, 2, rows, devices, width), (3, 0, 1, 2, 4))
    return pl.pallas_call(
        functools.partial(pack_kernel, start),
        in_specs=[pl.BlockSpec(memory_space=pltpu.HBM)] * 2,
        out_specs=pl.BlockSpec(memory_space=pltpu.HBM),
        out_shape=jax.ShapeDtypeStruct((devices, 2, 2, rows, width), jnp.bfloat16),
        scratch_shapes=[
            pltpu.VMEM((devices, 2, 2, rows, width), jnp.bfloat16),
            pltpu.SemaphoreType.DMA((2 * devices,)),
            pltpu.SemaphoreType.DMA((2 * devices,)),
        ],
        compiler_params=pltpu.CompilerParams(vmem_limit_bytes=48 * 2**20),
        cost_estimate=pl.CostEstimate(
            flops=0, bytes_accessed=devices * width * rows * 16, transcendentals=0
        ),
        name="pack",
    )(lesser, greater)


def unpack_kernel(start, *refs):
    received, (out, buffer, arrived, left) = refs[0], refs[-4:]
    devices, _, _, width = received.shape
    pairs = []
    for index in range(devices):
        columns = pl.ds(start + index * width, width)
        pairs.append((received.at[index], buffer.at[index], out.at[0, :, :, columns]))
    stage(pairs, arrived, left)


def unpack(received, start, total, result):
    devices, _, rows, width = received.shape
    more = {} if result is None else {"input_output_aliases": {1: 0}}
    held = [] if result is None else [result]
    return pl.pallas_call(
        functools.partial(unpack_kernel, start),
        in_specs=[pl.BlockSpec(memory_space=pltpu.HBM)] * (1 + len(held)),
        out_specs=pl.BlockSpec(memory_space=pltpu.HBM),
        out_shape=jax.ShapeDtypeStruct((1, 2, rows, total), jnp.bfloat16),
        scratch_shapes=[
            pltpu.VMEM(received.shape, jnp.bfloat16),
            pltpu.SemaphoreType.DMA((devices,)),
            pltpu.SemaphoreType.DMA((devices,)),
        ],
        compiler_params=pltpu.CompilerParams(vmem_limit_bytes=48 * 2**20),
        cost_estimate=pl.CostEstimate(
            flops=0, bytes_accessed=devices * width * rows * 8, transcendentals=0
        ),
        name="unpack",
        **more,
    )(received, *held)


def exchange(array):
    return lax.all_to_all(array, AXES, split_axis=0, concat_axis=0, tiled=True)


def after(value, *earlier):
    return lax.optimization_barrier((value, *earlier))[0]


def screen(near, coulomb, tile_block):
    tiles_n, block = coulomb.shape[1], coulomb.shape[2]
    levels = near.shape[2]
    band = (tiles_n + 2) // 3
    tiles = near.reshape(tiles_n, block, 2, levels, block)
    labels = jnp.arange(tiles_n, dtype=jnp.int32)
    onehot = tile_block[:, None] == labels[None, :]
    inverse = jnp.sum(jnp.where(onehot, labels[:, None], 0), axis=0)
    ordered = jnp.take(tiles, inverse, axis=0)
    results = []
    for r in range(band):
        for c in range(max(0, r - 1), min(band, r + 2)):
            inner = [l for l in range(max(0, r - 1), min(band, r + 2)) if abs(l - c) <= 1]
            acc = sum(
                jnp.einsum(
                    "ij,jsek->seik",
                    coulomb[0, 2 * r + l],
                    ordered[2 * l + c],
                    preferred_element_type=jnp.float32,
                )
                for l in inner
            )
            results.append(acc)
    return jnp.stack(results, axis=2).reshape(1, 2, levels, tiles_n * block * block)


def shards(lesser, greater, coulomb, tile_block, shift_table):
    count = lax.axis_size("mom")
    groups = lax.axis_size("energy")
    devices = count * groups
    rows, total = lesser.shape[2:]
    energies = rows * groups
    leading = energies // 4 // groups
    block = coulomb.shape[2]
    columns = total // devices
    chunks = 2 if columns % (2 * LANES) == 0 else 1
    width = columns // chunks
    direct = rows % 16 == 0
    forward, backward = (jnp.asarray(t) for t in tables(energies, 1.0 / math.sqrt(count * energies)))

    received, previous = [], None
    for chunk in range(chunks):
        sent = pack(lesser, greater, chunk * devices * width, width, devices)
        if previous is not None:
            sent = after(sent, previous)
        previous = exchange(sent)
        received.append(previous)

    outs, firsts, polar = [], [], None
    for chunk in range(chunks):
        data = received[chunk].reshape(groups, count, 2, 2, rows, width)
        if not direct:
            data = jnp.transpose(data, (1, 2, 3, 0, 4, 5)).reshape(1, count, 2, 2, energies, width)
        polar = correlate(data, shift_table, forward, backward)
        if not direct:
            polar = polar.reshape(count, 2, groups, rows, width)
            polar = jnp.transpose(polar, (2, 0, 1, 3, 4))
        outs.append(polar.reshape(devices, 2, rows, width))
        if leading:
            head = jnp.transpose(polar[: groups // 4], (1, 2, 0, 3, 4))
            head = head.reshape(count, 2, groups, leading, width)
            firsts.append(jnp.transpose(head, (2, 0, 1, 3, 4)).reshape(devices, 2, leading, width))

    results = []
    for chunk in range(chunks):
        if chunk == chunks - 1:
            first = jnp.concatenate(firsts, axis=3)
            first = after(first, previous)
            previous = near = exchange(first)
        previous = exchange(after(outs[chunk], previous))
        results.append(previous)

    polarization = None
    for chunk in range(chunks):
        if direct:
            polarization = unpack(results[chunk], chunk * devices * width, total, polarization)
    if not direct:
        pieces = jnp.stack(results)
        polarization = jnp.transpose(pieces, (2, 3, 0, 1, 4)).reshape(1, 2, rows, total)
    near = near.reshape(devices, 2, leading, chunks, width // block, block)
    near = jnp.transpose(near, (3, 0, 4, 1, 2, 5)).reshape(total // block, 2, leading, block)
    return (polarization, screen(near, coulomb, tile_block))


def solution(mesh):
    return jax.shard_map(
        shards,
        mesh=mesh,
        in_specs=(
            P("mom", None, "energy", None),
            P("mom", None, "energy", None),
            P("mom", None, None, None),
            P(),
            P(),
        ),
        out_specs=(P("mom", None, "energy", None), P("mom", None, "energy", None)),
        check_vma=False,
    )
```

```python
import functools
import math

import jax
import jax.numpy as jnp
import ml_dtypes
import numpy as np
from jax import lax
from jax.experimental import pallas as pl
from jax.experimental.pallas import tpu as pltpu
from jax.sharding import PartitionSpec as P

AXES = ("energy", "mom")
LANES = 128
FIRST = 3


def split_table(table):
    high = table.astype(np.float32).astype(ml_dtypes.bfloat16)
    low = (table - high.astype(np.float64)).astype(np.float32).astype(ml_dtypes.bfloat16)
    return high, low


@functools.lru_cache(maxsize=None)
def tables(energies, scale):
    period = 2 * energies
    turns = (2 * np.arange(energies)[:, None] + 1) * np.arange(energies)[None, :] % (2 * period)
    angle = np.pi / period * turns
    forward = np.concatenate((np.cos(angle), -np.sin(angle)), axis=0)
    backward = np.concatenate((np.cos(angle).T, -np.sin(angle).T), axis=1) * (scale / period)
    f_high, f_low = split_table(forward)
    b_high, b_low = split_table(backward)
    return np.concatenate((f_high, f_low), axis=1), np.concatenate((b_high, b_low, b_high), axis=1)


def correlate_kernel(shift, forward, backward, data, out, spectra, packed):
    blocks, count, _, _, rows, width = data.shape
    energies = blocks * rows

    def spectrum(index, carry):
        k, side, part = index // 4, index // 2 % 2, index % 2
        column = data[:, k, side, part].reshape(energies, width)
        both = jnp.concatenate((column, column), axis=0)
        spectra[index] = jnp.dot(forward[...], both, preferred_element_type=jnp.float32)
        return carry

    lax.fori_loop(0, 4 * count, spectrum, 0)
    step = 16

    def multiply(index, carry):
        row = pl.multiple_of(index * step, step)

        def load(k, side):
            base = (k * 2 + side) * 2
            a_re = spectra[base, pl.ds(row, step)]
            a_im = spectra[base, pl.ds(energies + row, step)]
            b_re = spectra[base + 1, pl.ds(row, step)]
            b_im = spectra[base + 1, pl.ds(energies + row, step)]
            return a_re - b_im, a_im + b_re, a_re + b_im, a_im - b_re

        left = [load(k, 0) for k in range(count)]
        for q in range(count):
            p_re = p_im = m_re = m_im = 0.0
            for k in range(count):
                lu_re, lu_im, lv_re, lv_im = left[k]
                ru_re, ru_im, rv_re, rv_im = load(shift[q, k], 1)
                p_re = p_re + lu_re * ru_re + lu_im * ru_im
                p_im = p_im + lu_im * ru_re - lu_re * ru_im
                m_re = m_re + lv_re * rv_re + lv_im * rv_im
                m_im = m_im + lv_im * rv_re - lv_re * rv_im
            parts = ((m_im - p_im, p_re - m_re), (p_re + m_re, p_im + m_im))
            for part in range(2):
                for half in range(2):
                    value = parts[part][half]
                    high = value.astype(jnp.bfloat16)
                    low = (value - high.astype(jnp.float32)).astype(jnp.bfloat16)
                    packed[2 * q + part, pl.ds(half * energies + row, step)] = high
                    packed[2 * q + part, pl.ds((2 + half) * energies + row, step)] = high
                    packed[2 * q + part, pl.ds((4 + half) * energies + row, step)] = low
        return carry

    lax.fori_loop(0, energies // step, multiply, 0)

    def invert(index, carry):
        result = jnp.dot(backward[...], packed[index], preferred_element_type=jnp.float32)
        out[:, index // 2, index % 2] = result.astype(jnp.bfloat16).reshape(blocks, rows, width)
        return carry

    lax.fori_loop(0, 2 * count, invert, 0)


def correlate(data, shift_table, forward, backward):
    blocks, count, _, _, rows, columns = data.shape
    energies = blocks * rows
    width = 256 if columns % 256 == 0 else columns
    work = 2 * columns * energies * energies * (16 * count + 12 * count)
    return pl.pallas_call(
        correlate_kernel,
        grid=(columns // width,),
        in_specs=[
            pl.BlockSpec(memory_space=pltpu.SMEM),
            pl.BlockSpec(forward.shape, lambda i: (0, 0)),
            pl.BlockSpec(backward.shape, lambda i: (0, 0)),
            pl.BlockSpec((blocks, count, 2, 2, rows, width), lambda i: (0, 0, 0, 0, 0, i)),
        ],
        out_specs=pl.BlockSpec((blocks, count, 2, rows, width), lambda i: (0, 0, 0, 0, i)),
        out_shape=jax.ShapeDtypeStruct((blocks, count, 2, rows, columns), jnp.bfloat16),
        scratch_shapes=[
            pltpu.VMEM((4 * count, 2 * energies, width), jnp.float32),
            pltpu.VMEM((2 * count, 6 * energies, width), jnp.bfloat16),
        ],
        compiler_params=pltpu.CompilerParams(vmem_limit_bytes=48 * 2**20),
        cost_estimate=pl.CostEstimate(
            flops=work, bytes_accessed=data.size * 3, transcendentals=0
        ),
        name="correlate",
    )(shift_table, forward, backward, data)


def stage(pairs, arrived, left):
    inward = [
        pltpu.make_async_copy(source, buffer, arrived.at[index])
        for index, (source, buffer, _) in enumerate(pairs)
    ]
    outward = [
        pltpu.make_async_copy(buffer, target, left.at[index])
        for index, (_, buffer, target) in enumerate(pairs)
    ]
    for copy in inward:
        copy.start()
    for first, second in zip(inward, outward):
        first.wait()
        second.start()
    for copy in outward:
        copy.wait()


def pack_kernel(start, lesser, greater, out, buffer, arrived, left):
    devices, _, _, _, width = out.shape
    pairs = []
    for index in range(devices):
        columns = pl.ds(start + index * width, width)
        for side, array in enumerate((lesser, greater)):
            pairs.append((array.at[0, :, :, columns], buffer.at[index, side], out.at[index, side]))
    stage(pairs, arrived, left)


def pack(lesser, greater, start, width, devices):
    _, _, rows, _ = lesser.shape
    if rows % 16 or width % LANES or devices > 64:
        both = jnp.concatenate((lesser, greater), axis=0)[..., start : start + devices * width]
        return jnp.transpose(both.reshape(2, 2, rows, devices, width), (3, 0, 1, 2, 4))
    return pl.pallas_call(
        functools.partial(pack_kernel, start),
        in_specs=[pl.BlockSpec(memory_space=pltpu.HBM)] * 2,
        out_specs=pl.BlockSpec(memory_space=pltpu.HBM),
        out_shape=jax.ShapeDtypeStruct((devices, 2, 2, rows, width), jnp.bfloat16),
        scratch_shapes=[
            pltpu.VMEM((devices, 2, 2, rows, width), jnp.bfloat16),
            pltpu.SemaphoreType.DMA((2 * devices,)),
            pltpu.SemaphoreType.DMA((2 * devices,)),
        ],
        compiler_params=pltpu.CompilerParams(vmem_limit_bytes=48 * 2**20),
        cost_estimate=pl.CostEstimate(
            flops=0, bytes_accessed=devices * width * rows * 16, transcendentals=0
        ),
        name="pack",
    )(lesser, greater)


def unpack_kernel(start, *refs):
    received, (out, buffer, arrived, left) = refs[0], refs[-4:]
    devices, _, _, width = received.shape
    pairs = []
    for index in range(devices):
        columns = pl.ds(start + index * width, width)
        pairs.append((received.at[index], buffer.at[index], out.at[0, :, :, columns]))
    stage(pairs, arrived, left)


def unpack(received, start, total, result):
    devices, _, rows, width = received.shape
    more = {} if result is None else {"input_output_aliases": {1: 0}}
    held = [] if result is None else [result]
    return pl.pallas_call(
        functools.partial(unpack_kernel, start),
        in_specs=[pl.BlockSpec(memory_space=pltpu.HBM)] * (1 + len(held)),
        out_specs=pl.BlockSpec(memory_space=pltpu.HBM),
        out_shape=jax.ShapeDtypeStruct((1, 2, rows, total), jnp.bfloat16),
        scratch_shapes=[
            pltpu.VMEM(received.shape, jnp.bfloat16),
            pltpu.SemaphoreType.DMA((devices,)),
            pltpu.SemaphoreType.DMA((devices,)),
        ],
        compiler_params=pltpu.CompilerParams(vmem_limit_bytes=48 * 2**20),
        cost_estimate=pl.CostEstimate(
            flops=0, bytes_accessed=devices * width * rows * 8, transcendentals=0
        ),
        name="unpack",
        **more,
    )(received, *held)


def exchange(array):
    return lax.all_to_all(array, AXES, split_axis=0, concat_axis=0, tiled=True)


def after(value, *earlier):
    return lax.optimization_barrier((value, *earlier))[0]


def screen(near, coulomb, tile_block):
    tiles_n, block = coulomb.shape[1], coulomb.shape[2]
    levels = near.shape[2]
    band = (tiles_n + 2) // 3
    tiles = near.reshape(tiles_n, block, 2, levels, block)
    labels = jnp.arange(tiles_n, dtype=jnp.int32)
    onehot = tile_block[:, None] == labels[None, :]
    inverse = jnp.sum(jnp.where(onehot, labels[:, None], 0), axis=0)
    ordered = jnp.take(tiles, inverse, axis=0)
    results = []
    for r in range(band):
        for c in range(max(0, r - 1), min(band, r + 2)):
            inner = [l for l in range(max(0, r - 1), min(band, r + 2)) if abs(l - c) <= 1]
            acc = sum(
                jnp.einsum(
                    "ij,jsek->seik",
                    coulomb[0, 2 * r + l],
                    ordered[2 * l + c],
                    preferred_element_type=jnp.float32,
                )
                for l in inner
            )
            results.append(acc)
    return jnp.stack(results, axis=2).reshape(1, 2, levels, tiles_n * block * block)


def chunk_widths(columns):
    step = 2 * LANES
    if columns % step or columns < 2 * step:
        return [columns] if columns % (2 * LANES) else [columns // 2] * 2
    first = columns // step * FIRST // 8 * step
    return [first, columns - first]


def shards(lesser, greater, coulomb, tile_block, shift_table):
    count = lax.axis_size("mom")
    groups = lax.axis_size("energy")
    devices = count * groups
    rows, total = lesser.shape[2:]
    energies = rows * groups
    leading = energies // 4 // groups
    block = coulomb.shape[2]
    columns = total // devices
    widths = chunk_widths(columns)
    starts = [devices * sum(widths[:chunk]) for chunk in range(len(widths))]
    direct = rows % 16 == 0
    forward, backward = (jnp.asarray(t) for t in tables(energies, 1.0 / math.sqrt(count * energies)))

    received, previous = [], None
    for start, width in zip(starts, widths):
        sent = pack(lesser, greater, start, width, devices)
        if previous is not None:
            sent = after(sent, previous)
        previous = exchange(sent)
        received.append(previous)

    outs, firsts = [], []
    for data, width in zip(received, widths):
        data = data.reshape(groups, count, 2, 2, rows, width)
        if not direct:
            data = jnp.transpose(data, (1, 2, 3, 0, 4, 5)).reshape(1, count, 2, 2, energies, width)
        polar = correlate(data, shift_table, forward, backward)
        if not direct:
            polar = polar.reshape(count, 2, groups, rows, width)
            polar = jnp.transpose(polar, (2, 0, 1, 3, 4))
        outs.append(polar.reshape(devices, 2, rows, width))
        head = jnp.transpose(polar[: groups // 4], (1, 2, 0, 3, 4))
        head = head.reshape(count, 2, groups, leading, width)
        firsts.append(jnp.transpose(head, (2, 0, 1, 3, 4)).reshape(devices, 2, leading, width))

    results = []
    for chunk, out in enumerate(outs):
        if chunk == len(outs) - 1:
            previous = first = exchange(after(jnp.concatenate(firsts, axis=3), previous))
        previous = exchange(after(out, previous))
        results.append(previous)

    polarization = None
    for result, start in zip(results, starts):
        if direct:
            polarization = unpack(result, start, total, polarization)
    if not direct:
        pieces = [jnp.transpose(result, (1, 2, 0, 3)).reshape(2, rows, -1) for result in results]
        polarization = jnp.concatenate(pieces, axis=2)[None]
    near = []
    for chunk, width in enumerate(widths):
        part = first[..., sum(widths[:chunk]) : sum(widths[: chunk + 1])]
        part = part.reshape(devices, 2, leading, width // block, block)
        near.append(jnp.transpose(part, (0, 3, 1, 2, 4)).reshape(-1, 2, leading, block))
    return (polarization, screen(jnp.concatenate(near), coulomb, tile_block))


def solution(mesh):
    return jax.shard_map(
        shards,
        mesh=mesh,
        in_specs=(
            P("mom", None, "energy", None),
            P("mom", None, "energy", None),
            P("mom", None, None, None),
            P(),
            P(),
        ),
        out_specs=(P("mom", None, "energy", None), P("mom", None, "energy", None)),
        check_vma=False,
    )
```

```python
import functools
import math

import jax
import jax.numpy as jnp
import ml_dtypes
import numpy as np
from jax import lax
from jax.experimental import pallas as pl
from jax.experimental.pallas import tpu as pltpu
from jax.sharding import PartitionSpec as P

AXES = ("energy", "mom")
LANES = 128
FIRST = 4


def split_table(table):
    high = table.astype(np.float32).astype(ml_dtypes.bfloat16)
    low = (table - high.astype(np.float64)).astype(np.float32).astype(ml_dtypes.bfloat16)
    return high, low


@functools.lru_cache(maxsize=None)
def tables(energies, scale):
    period = 2 * energies
    turns = (2 * np.arange(energies)[:, None] + 1) * np.arange(energies)[None, :] % (2 * period)
    angle = np.pi / period * turns
    forward = np.concatenate((np.cos(angle), -np.sin(angle)), axis=0)
    backward = np.concatenate((np.cos(angle).T, -np.sin(angle).T), axis=1) * (scale / period)
    f_high, f_low = split_table(forward)
    b_high, b_low = split_table(backward)
    return np.concatenate((f_high, f_low), axis=1), np.concatenate((b_high, b_low, b_high), axis=1)


def correlate_kernel(shift, forward, backward, data, out, spectra, packed):
    blocks, count, _, _, rows, width = data.shape
    energies = blocks * rows

    def spectrum(index, carry):
        k, side, part = index // 4, index // 2 % 2, index % 2
        column = data[:, k, side, part].reshape(energies, width)
        both = jnp.concatenate((column, column), axis=0)
        spectra[index] = jnp.dot(forward[...], both, preferred_element_type=jnp.float32)
        return carry

    lax.fori_loop(0, 4 * count, spectrum, 0)
    step = 16

    def multiply(index, carry):
        row = pl.multiple_of(index * step, step)

        def load(k, side):
            base = (k * 2 + side) * 2
            a_re = spectra[base, pl.ds(row, step)]
            a_im = spectra[base, pl.ds(energies + row, step)]
            b_re = spectra[base + 1, pl.ds(row, step)]
            b_im = spectra[base + 1, pl.ds(energies + row, step)]
            return a_re - b_im, a_im + b_re, a_re + b_im, a_im - b_re

        left = [load(k, 0) for k in range(count)]
        for q in range(count):
            p_re = p_im = m_re = m_im = 0.0
            for k in range(count):
                lu_re, lu_im, lv_re, lv_im = left[k]
                ru_re, ru_im, rv_re, rv_im = load(shift[q, k], 1)
                p_re = p_re + lu_re * ru_re + lu_im * ru_im
                p_im = p_im + lu_im * ru_re - lu_re * ru_im
                m_re = m_re + lv_re * rv_re + lv_im * rv_im
                m_im = m_im + lv_im * rv_re - lv_re * rv_im
            parts = ((m_im - p_im, p_re - m_re), (p_re + m_re, p_im + m_im))
            for part in range(2):
                for half in range(2):
                    value = parts[part][half]
                    high = value.astype(jnp.bfloat16)
                    low = (value - high.astype(jnp.float32)).astype(jnp.bfloat16)
                    packed[2 * q + part, pl.ds(half * energies + row, step)] = high
                    packed[2 * q + part, pl.ds((2 + half) * energies + row, step)] = high
                    packed[2 * q + part, pl.ds((4 + half) * energies + row, step)] = low
        return carry

    lax.fori_loop(0, energies // step, multiply, 0)

    def invert(index, carry):
        result = jnp.dot(backward[...], packed[index], preferred_element_type=jnp.float32)
        out[:, index // 2, index % 2] = result.astype(jnp.bfloat16).reshape(blocks, rows, width)
        return carry

    lax.fori_loop(0, 2 * count, invert, 0)


def correlate(data, shift_table, forward, backward):
    blocks, count, _, _, rows, columns = data.shape
    energies = blocks * rows
    width = 256 if columns % 256 == 0 else columns
    work = 2 * columns * energies * energies * (16 * count + 12 * count)
    return pl.pallas_call(
        correlate_kernel,
        grid=(columns // width,),
        in_specs=[
            pl.BlockSpec(memory_space=pltpu.SMEM),
            pl.BlockSpec(forward.shape, lambda i: (0, 0)),
            pl.BlockSpec(backward.shape, lambda i: (0, 0)),
            pl.BlockSpec((blocks, count, 2, 2, rows, width), lambda i: (0, 0, 0, 0, 0, i)),
        ],
        out_specs=pl.BlockSpec((blocks, count, 2, rows, width), lambda i: (0, 0, 0, 0, i)),
        out_shape=jax.ShapeDtypeStruct((blocks, count, 2, rows, columns), jnp.bfloat16),
        scratch_shapes=[
            pltpu.VMEM((4 * count, 2 * energies, width), jnp.float32),
            pltpu.VMEM((2 * count, 6 * energies, width), jnp.bfloat16),
        ],
        compiler_params=pltpu.CompilerParams(vmem_limit_bytes=48 * 2**20),
        cost_estimate=pl.CostEstimate(
            flops=work, bytes_accessed=data.size * 3, transcendentals=0
        ),
        name="correlate",
    )(shift_table, forward, backward, data)


def stage(pairs, arrived, left):
    inward = [
        pltpu.make_async_copy(source, buffer, arrived.at[index])
        for index, (source, buffer, _) in enumerate(pairs)
    ]
    outward = [
        pltpu.make_async_copy(buffer, target, left.at[index])
        for index, (_, buffer, target) in enumerate(pairs)
    ]
    for copy in inward:
        copy.start()
    for first, second in zip(inward, outward):
        first.wait()
        second.start()
    for copy in outward:
        copy.wait()


def pack_kernel(start, lesser, greater, out, buffer, arrived, left):
    devices, _, _, _, width = out.shape
    pairs = []
    for index in range(devices):
        columns = pl.ds(start + index * width, width)
        for side, array in enumerate((lesser, greater)):
            pairs.append((array.at[0, :, :, columns], buffer.at[index, side], out.at[index, side]))
    stage(pairs, arrived, left)


def pack(lesser, greater, start, width, devices):
    _, _, rows, _ = lesser.shape
    if rows % 16 or width % LANES or devices > 64:
        both = jnp.concatenate((lesser, greater), axis=0)[..., start : start + devices * width]
        return jnp.transpose(both.reshape(2, 2, rows, devices, width), (3, 0, 1, 2, 4))
    return pl.pallas_call(
        functools.partial(pack_kernel, start),
        in_specs=[pl.BlockSpec(memory_space=pltpu.HBM)] * 2,
        out_specs=pl.BlockSpec(memory_space=pltpu.HBM),
        out_shape=jax.ShapeDtypeStruct((devices, 2, 2, rows, width), jnp.bfloat16),
        scratch_shapes=[
            pltpu.VMEM((devices, 2, 2, rows, width), jnp.bfloat16),
            pltpu.SemaphoreType.DMA((2 * devices,)),
            pltpu.SemaphoreType.DMA((2 * devices,)),
        ],
        compiler_params=pltpu.CompilerParams(vmem_limit_bytes=48 * 2**20),
        cost_estimate=pl.CostEstimate(
            flops=0, bytes_accessed=devices * width * rows * 16, transcendentals=0
        ),
        name="pack",
    )(lesser, greater)


def unpack_kernel(start, stride, offset, *refs):
    received, (out, buffer, arrived, left) = refs[0], refs[-4:]
    devices, _, rows, width = buffer.shape
    pairs = []
    for index in range(devices):
        columns = pl.ds(start + index * stride + offset, width)
        source = received.at[index, :, pl.ds(0, rows)]
        pairs.append((source, buffer.at[index], out.at[0, :, :, columns]))
    stage(pairs, arrived, left)


def unpack(received, rows, start, stride, offset, total, result):
    devices, _, _, width = received.shape
    more = {} if result is None else {"input_output_aliases": {1: 0}}
    held = [] if result is None else [result]
    return pl.pallas_call(
        functools.partial(unpack_kernel, start, stride, offset),
        in_specs=[pl.BlockSpec(memory_space=pltpu.HBM)] * (1 + len(held)),
        out_specs=pl.BlockSpec(memory_space=pltpu.HBM),
        out_shape=jax.ShapeDtypeStruct((1, 2, rows, total), jnp.bfloat16),
        scratch_shapes=[
            pltpu.VMEM((devices, 2, rows, width), jnp.bfloat16),
            pltpu.SemaphoreType.DMA((devices,)),
            pltpu.SemaphoreType.DMA((devices,)),
        ],
        compiler_params=pltpu.CompilerParams(vmem_limit_bytes=48 * 2**20),
        cost_estimate=pl.CostEstimate(
            flops=0, bytes_accessed=devices * width * rows * 8, transcendentals=0
        ),
        name="unpack",
        **more,
    )(received, *held)


def exchange(array):
    return lax.all_to_all(array, AXES, split_axis=0, concat_axis=0, tiled=True)


def after(value, *earlier):
    return lax.optimization_barrier((value, *earlier))[0]


def screen(near, coulomb, tile_block):
    tiles_n, block = coulomb.shape[1], coulomb.shape[2]
    levels = near.shape[2]
    band = (tiles_n + 2) // 3
    tiles = near.reshape(tiles_n, block, 2, levels, block)
    labels = jnp.arange(tiles_n, dtype=jnp.int32)
    onehot = tile_block[:, None] == labels[None, :]
    inverse = jnp.sum(jnp.where(onehot, labels[:, None], 0), axis=0)
    ordered = jnp.take(tiles, inverse, axis=0)
    results = []
    for r in range(band):
        for c in range(max(0, r - 1), min(band, r + 2)):
            inner = [l for l in range(max(0, r - 1), min(band, r + 2)) if abs(l - c) <= 1]
            acc = sum(
                jnp.einsum(
                    "ij,jsek->seik",
                    coulomb[0, 2 * r + l],
                    ordered[2 * l + c],
                    preferred_element_type=jnp.float32,
                )
                for l in inner
            )
            results.append(acc)
    return jnp.stack(results, axis=2).reshape(1, 2, levels, tiles_n * block * block)


def chunk_widths(columns):
    step = 2 * LANES
    if columns % step or columns < 2 * step:
        return [columns] if columns % (2 * LANES) else [columns // 2] * 2
    first = columns // step * FIRST // 8 * step
    return [first, columns - first]


def shards(lesser, greater, coulomb, tile_block, shift_table):
    count = lax.axis_size("mom")
    groups = lax.axis_size("energy")
    devices = count * groups
    rows, total = lesser.shape[2:]
    energies = rows * groups
    leading = energies // 4 // groups
    block = coulomb.shape[2]
    columns = total // devices
    widths = chunk_widths(columns)
    starts = [devices * sum(widths[:chunk]) for chunk in range(len(widths))]
    direct = rows % 16 == 0
    forward, backward = (jnp.asarray(t) for t in tables(energies, 1.0 / math.sqrt(count * energies)))

    received, previous = [], None
    for start, width in zip(starts, widths):
        sent = pack(lesser, greater, start, width, devices)
        if previous is not None:
            sent = after(sent, previous)
        previous = exchange(sent)
        received.append(previous)

    outs, firsts = [], []
    for data, width in zip(received, widths):
        data = data.reshape(groups, count, 2, 2, rows, width)
        if not direct:
            data = jnp.transpose(data, (1, 2, 3, 0, 4, 5)).reshape(1, count, 2, 2, energies, width)
        polar = correlate(data, shift_table, forward, backward)
        if not direct:
            polar = polar.reshape(count, 2, groups, rows, width)
            polar = jnp.transpose(polar, (2, 0, 1, 3, 4))
        outs.append(polar.reshape(devices, 2, rows, width))
        head = jnp.transpose(polar[: groups // 4], (1, 2, 0, 3, 4))
        head = head.reshape(count, 2, groups, leading, width)
        firsts.append(jnp.transpose(head, (2, 0, 1, 3, 4)).reshape(devices, 2, leading, width))

    results = []
    half = widths[-1] // 2
    merge = direct and half % LANES == 0 and columns % half == 0
    for chunk, out in enumerate(outs):
        if chunk == len(outs) - 1:
            first = jnp.concatenate(firsts, axis=3)
            if merge:
                first = first.reshape(devices, 2, leading, columns // half, half)
                first = jnp.transpose(first, (0, 1, 3, 2, 4)).reshape(devices, 2, -1, half)
                first = jnp.concatenate((out[..., :half], first), axis=2)
            previous = first = exchange(after(first, previous))
            if merge:
                results.append(first)
                first = first[:, :, rows:].reshape(devices, 2, columns // half, leading, half)
                first = jnp.transpose(first, (0, 1, 3, 2, 4)).reshape(devices, 2, leading, columns)
                out = out[..., half:]
        previous = exchange(after(out, previous))
        results.append(previous)

    polarization = None
    if direct:
        step = 0
        for chunk, result in enumerate(results):
            last = chunk >= len(widths) - 1
            polarization = unpack(
                result, rows, starts[min(chunk, len(widths) - 1)], widths[min(chunk, len(widths) - 1)],
                step, total, polarization,
            )
            step += result.shape[3] if last else 0
    else:
        pieces = [jnp.transpose(result, (1, 2, 0, 3)).reshape(2, rows, -1) for result in results]
        polarization = jnp.concatenate(pieces, axis=2)[None]
    near = []
    for chunk, width in enumerate(widths):
        part = first[..., sum(widths[:chunk]) : sum(widths[: chunk + 1])]
        part = part.reshape(devices, 2, leading, width // block, block)
        near.append(jnp.transpose(part, (0, 3, 1, 2, 4)).reshape(-1, 2, leading, block))
    return (polarization, screen(jnp.concatenate(near), coulomb, tile_block))


def solution(mesh):
    return jax.shard_map(
        shards,
        mesh=mesh,
        in_specs=(
            P("mom", None, "energy", None),
            P("mom", None, "energy", None),
            P("mom", None, None, None),
            P(),
            P(),
        ),
        out_specs=(P("mom", None, "energy", None), P("mom", None, "energy", None)),
        check_vma=False,
    )
```

```python
import functools
import math

import jax
import jax.numpy as jnp
import ml_dtypes
import numpy as np
from jax import lax
from jax.experimental import pallas as pl
from jax.experimental.pallas import tpu as pltpu
from jax.sharding import PartitionSpec as P

AXES = ("energy", "mom")
LANES = 128
FIRST = 4


def split_table(table):
    high = table.astype(np.float32).astype(ml_dtypes.bfloat16)
    low = (table - high.astype(np.float64)).astype(np.float32).astype(ml_dtypes.bfloat16)
    return high, low


@functools.lru_cache(maxsize=None)
def tables(energies, scale):
    period = 2 * energies
    turns = (2 * np.arange(energies)[:, None] + 1) * np.arange(energies)[None, :] % (2 * period)
    angle = np.pi / period * turns
    forward = np.concatenate((np.cos(angle), -np.sin(angle)), axis=0)
    backward = np.concatenate((np.cos(angle).T, -np.sin(angle).T), axis=1) * (scale / period)
    f_high, f_low = split_table(forward)
    b_high, b_low = split_table(backward)
    return np.concatenate((f_high, f_low), axis=1), np.concatenate((b_high, b_low, b_high), axis=1)


def correlate_kernel(shift, forward, backward, data, out, spectra, packed):
    blocks, count, _, _, rows, width = data.shape
    energies = blocks * rows

    def spectrum(index, carry):
        k, side, part = index // 4, index // 2 % 2, index % 2
        column = data[:, k, side, part].reshape(energies, width)
        both = jnp.concatenate((column, column), axis=0)
        spectra[index] = jnp.dot(forward[...], both, preferred_element_type=jnp.float32)
        return carry

    lax.fori_loop(0, 4 * count, spectrum, 0)
    step = 16

    def multiply(index, carry):
        row = pl.multiple_of(index * step, step)

        def load(k, side):
            base = (k * 2 + side) * 2
            a_re = spectra[base, pl.ds(row, step)]
            a_im = spectra[base, pl.ds(energies + row, step)]
            b_re = spectra[base + 1, pl.ds(row, step)]
            b_im = spectra[base + 1, pl.ds(energies + row, step)]
            return a_re - b_im, a_im + b_re, a_re + b_im, a_im - b_re

        left = [load(k, 0) for k in range(count)]
        for q in range(count):
            p_re = p_im = m_re = m_im = 0.0
            for k in range(count):
                lu_re, lu_im, lv_re, lv_im = left[k]
                ru_re, ru_im, rv_re, rv_im = load(shift[q, k], 1)
                p_re = p_re + lu_re * ru_re + lu_im * ru_im
                p_im = p_im + lu_im * ru_re - lu_re * ru_im
                m_re = m_re + lv_re * rv_re + lv_im * rv_im
                m_im = m_im + lv_im * rv_re - lv_re * rv_im
            parts = ((m_im - p_im, p_re - m_re), (p_re + m_re, p_im + m_im))
            for part in range(2):
                for half in range(2):
                    value = parts[part][half]
                    high = value.astype(jnp.bfloat16)
                    low = (value - high.astype(jnp.float32)).astype(jnp.bfloat16)
                    packed[2 * q + part, pl.ds(half * energies + row, step)] = high
                    packed[2 * q + part, pl.ds((2 + half) * energies + row, step)] = high
                    packed[2 * q + part, pl.ds((4 + half) * energies + row, step)] = low
        return carry

    lax.fori_loop(0, energies // step, multiply, 0)

    def invert(index, carry):
        result = jnp.dot(backward[...], packed[index], preferred_element_type=jnp.float32)
        out[:, index // 2, index % 2] = result.astype(jnp.bfloat16).reshape(blocks, rows, width)
        return carry

    lax.fori_loop(0, 2 * count, invert, 0)


def correlate(data, shift_table, forward, backward):
    blocks, count, _, _, rows, columns = data.shape
    energies = blocks * rows
    width = 256 if columns % 256 == 0 else columns
    work = 2 * columns * energies * energies * (16 * count + 12 * count)
    return pl.pallas_call(
        correlate_kernel,
        grid=(columns // width,),
        in_specs=[
            pl.BlockSpec(memory_space=pltpu.SMEM),
            pl.BlockSpec(forward.shape, lambda i: (0, 0)),
            pl.BlockSpec(backward.shape, lambda i: (0, 0)),
            pl.BlockSpec((blocks, count, 2, 2, rows, width), lambda i: (0, 0, 0, 0, 0, i)),
        ],
        out_specs=pl.BlockSpec((blocks, count, 2, rows, width), lambda i: (0, 0, 0, 0, i)),
        out_shape=jax.ShapeDtypeStruct((blocks, count, 2, rows, columns), jnp.bfloat16),
        scratch_shapes=[
            pltpu.VMEM((4 * count, 2 * energies, width), jnp.float32),
            pltpu.VMEM((2 * count, 6 * energies, width), jnp.bfloat16),
        ],
        compiler_params=pltpu.CompilerParams(vmem_limit_bytes=48 * 2**20),
        cost_estimate=pl.CostEstimate(
            flops=work, bytes_accessed=data.size * 3, transcendentals=0
        ),
        name="correlate",
    )(shift_table, forward, backward, data)


def stage(pairs, arrived, left):
    inward = [
        pltpu.make_async_copy(source, buffer, arrived.at[index])
        for index, (source, buffer, _) in enumerate(pairs)
    ]
    outward = [
        pltpu.make_async_copy(buffer, target, left.at[index])
        for index, (_, buffer, target) in enumerate(pairs)
    ]
    for copy in inward:
        copy.start()
    for first, second in zip(inward, outward):
        first.wait()
        second.start()
    for copy in outward:
        copy.wait()


def pack_kernel(start, lesser, greater, out, buffer, arrived, left):
    devices, _, _, _, width = out.shape
    inward, outward = [], []
    for index in range(devices):
        columns = pl.ds(start + index * width, width)
        for side, array in enumerate((lesser, greater)):
            source, signal = array.at[0, :, :, columns], arrived.at[2 * index + side]
            inward.append(pltpu.make_async_copy(source, buffer.at[index, side], signal))
        outward.append(pltpu.make_async_copy(buffer.at[index], out.at[index], left.at[index]))
    for copy in inward:
        copy.start()
    for index, copy in enumerate(outward):
        inward[2 * index].wait()
        inward[2 * index + 1].wait()
        copy.start()
    for copy in outward:
        copy.wait()


def pack(lesser, greater, start, width, devices):
    _, _, rows, _ = lesser.shape
    if rows % 16 or width % LANES or devices > 64:
        both = jnp.concatenate((lesser, greater), axis=0)[..., start : start + devices * width]
        return jnp.transpose(both.reshape(2, 2, rows, devices, width), (3, 0, 1, 2, 4))
    return pl.pallas_call(
        functools.partial(pack_kernel, start),
        in_specs=[pl.BlockSpec(memory_space=pltpu.HBM)] * 2,
        out_specs=pl.BlockSpec(memory_space=pltpu.HBM),
        out_shape=jax.ShapeDtypeStruct((devices, 2, 2, rows, width), jnp.bfloat16),
        scratch_shapes=[
            pltpu.VMEM((devices, 2, 2, rows, width), jnp.bfloat16),
            pltpu.SemaphoreType.DMA((2 * devices,)),
            pltpu.SemaphoreType.DMA((2 * devices,)),
        ],
        compiler_params=pltpu.CompilerParams(vmem_limit_bytes=48 * 2**20),
        cost_estimate=pl.CostEstimate(
            flops=0, bytes_accessed=devices * width * rows * 16, transcendentals=0
        ),
        name="pack",
    )(lesser, greater)


def unpack_kernel(start, stride, offset, *refs):
    received, (out, buffer, arrived, left) = refs[0], refs[-4:]
    devices, _, rows, width = buffer.shape
    pairs = []
    for index in range(devices):
        columns = pl.ds(start + index * stride + offset, width)
        source = received.at[index, :, pl.ds(0, rows)]
        pairs.append((source, buffer.at[index], out.at[0, :, :, columns]))
    stage(pairs, arrived, left)


def unpack(received, rows, start, stride, offset, total, result):
    devices, _, _, width = received.shape
    more = {} if result is None else {"input_output_aliases": {1: 0}}
    held = [] if result is None else [result]
    return pl.pallas_call(
        functools.partial(unpack_kernel, start, stride, offset),
        in_specs=[pl.BlockSpec(memory_space=pltpu.HBM)] * (1 + len(held)),
        out_specs=pl.BlockSpec(memory_space=pltpu.HBM),
        out_shape=jax.ShapeDtypeStruct((1, 2, rows, total), jnp.bfloat16),
        scratch_shapes=[
            pltpu.VMEM((devices, 2, rows, width), jnp.bfloat16),
            pltpu.SemaphoreType.DMA((devices,)),
            pltpu.SemaphoreType.DMA((devices,)),
        ],
        compiler_params=pltpu.CompilerParams(vmem_limit_bytes=48 * 2**20),
        cost_estimate=pl.CostEstimate(
            flops=0, bytes_accessed=devices * width * rows * 8, transcendentals=0
        ),
        name="unpack",
        **more,
    )(received, *held)


def exchange(array):
    return lax.all_to_all(array, AXES, split_axis=0, concat_axis=0, tiled=True)


def after(value, *earlier):
    return lax.optimization_barrier((value, *earlier))[0]


def screen(near, coulomb, tile_block):
    tiles_n, block = coulomb.shape[1], coulomb.shape[2]
    levels = near.shape[2]
    band = (tiles_n + 2) // 3
    tiles = near.reshape(tiles_n, block, 2, levels, block)
    labels = jnp.arange(tiles_n, dtype=jnp.int32)
    onehot = tile_block[:, None] == labels[None, :]
    inverse = jnp.sum(jnp.where(onehot, labels[:, None], 0), axis=0)
    ordered = jnp.take(tiles, inverse, axis=0)
    results = []
    for r in range(band):
        for c in range(max(0, r - 1), min(band, r + 2)):
            inner = [l for l in range(max(0, r - 1), min(band, r + 2)) if abs(l - c) <= 1]
            acc = sum(
                jnp.einsum(
                    "ij,jsek->seik",
                    coulomb[0, 2 * r + l],
                    ordered[2 * l + c],
                    preferred_element_type=jnp.float32,
                )
                for l in inner
            )
            results.append(acc)
    return jnp.stack(results, axis=2).reshape(1, 2, levels, tiles_n * block * block)


def chunk_widths(columns):
    step = 2 * LANES
    if columns % step or columns < 2 * step:
        return [columns] if columns % (2 * LANES) else [columns // 2] * 2
    first = columns // step * FIRST // 8 * step
    return [first, columns - first]


def shards(lesser, greater, coulomb, tile_block, shift_table):
    count = lax.axis_size("mom")
    groups = lax.axis_size("energy")
    devices = count * groups
    rows, total = lesser.shape[2:]
    energies = rows * groups
    leading = energies // 4 // groups
    block = coulomb.shape[2]
    columns = total // devices
    widths = chunk_widths(columns)
    starts = [devices * sum(widths[:chunk]) for chunk in range(len(widths))]
    direct = rows % 16 == 0
    forward, backward = (jnp.asarray(t) for t in tables(energies, 1.0 / math.sqrt(count * energies)))

    received, previous = [], None
    for start, width in zip(starts, widths):
        sent = pack(lesser, greater, start, width, devices)
        if previous is not None:
            sent = after(sent, previous)
        previous = exchange(sent)
        received.append(previous)

    outs, firsts = [], []
    for data, width in zip(received, widths):
        data = data.reshape(groups, count, 2, 2, rows, width)
        if not direct:
            data = jnp.transpose(data, (1, 2, 3, 0, 4, 5)).reshape(1, count, 2, 2, energies, width)
        polar = correlate(data, shift_table, forward, backward)
        if not direct:
            polar = polar.reshape(count, 2, groups, rows, width)
            polar = jnp.transpose(polar, (2, 0, 1, 3, 4))
        outs.append(polar.reshape(devices, 2, rows, width))
        head = jnp.transpose(polar[: groups // 4], (1, 2, 0, 3, 4))
        head = head.reshape(count, 2, groups, leading, width)
        firsts.append(jnp.transpose(head, (2, 0, 1, 3, 4)).reshape(devices, 2, leading, width))

    results = []
    half = widths[-1] // 2
    merge = direct and half % LANES == 0 and columns % half == 0
    for chunk, out in enumerate(outs):
        if chunk == len(outs) - 1:
            first = jnp.concatenate(firsts, axis=3)
            if merge:
                first = first.reshape(devices, 2, leading, columns // half, half)
                first = jnp.transpose(first, (0, 1, 3, 2, 4)).reshape(devices, 2, -1, half)
                first = jnp.concatenate((out[..., :half], first), axis=2)
            previous = first = exchange(after(first, previous))
            if merge:
                results.append(first)
                first = first[:, :, rows:].reshape(devices, 2, columns // half, leading, half)
                first = jnp.transpose(first, (0, 1, 3, 2, 4)).reshape(devices, 2, leading, columns)
                out = out[..., half:]
        previous = exchange(after(out, previous))
        results.append(previous)

    polarization = None
    if direct:
        step = 0
        for chunk, result in enumerate(results):
            last = chunk >= len(widths) - 1
            polarization = unpack(
                result, rows, starts[min(chunk, len(widths) - 1)], widths[min(chunk, len(widths) - 1)],
                step, total, polarization,
            )
            step += result.shape[3] if last else 0
    else:
        pieces = [jnp.transpose(result, (1, 2, 0, 3)).reshape(2, rows, -1) for result in results]
        polarization = jnp.concatenate(pieces, axis=2)[None]
    near = []
    for chunk, width in enumerate(widths):
        part = first[..., sum(widths[:chunk]) : sum(widths[: chunk + 1])]
        part = part.reshape(devices, 2, leading, width // block, block)
        near.append(jnp.transpose(part, (0, 3, 1, 2, 4)).reshape(-1, 2, leading, block))
    return (polarization, screen(jnp.concatenate(near), coulomb, tile_block))


def solution(mesh):
    return jax.shard_map(
        shards,
        mesh=mesh,
        in_specs=(
            P("mom", None, "energy", None),
            P("mom", None, "energy", None),
            P("mom", None, None, None),
            P(),
            P(),
        ),
        out_specs=(P("mom", None, "energy", None), P("mom", None, "energy", None)),
        check_vma=False,
    )
```
